512 devices in a mesh: ctx: 32 (over z, y_lo, core), dp: 16 (over y_hi, x).
Axes of the slice: x: 4, y: 8 (y_hi: 4, y_lo: 2; y = y_hi * 2 + y_lo), z: 8, core: 2. Of those that a mesh axis runs over, the one named last changes fastest.
Arguments:
- hidden: bfloat16 [16, 4096, 2048], P('dp', 'ctx')
- key_weight: bfloat16 [2048, 1024], P('ctx'), may hold values from -0.125 to 0.125
- cluster_ids: int32 [16, 8, 4096], P('dp', None, 'ctx'), may hold values from 0 to 511, as said below
- old_centroids: float32 [4096, 128], P(('ctx', 'dp')), may hold values from -6 to 6
Outputs:
- centroids: float32 [4096, 128], replicated
The draws below stay inside these ranges and needn't reach their ends.
Inputs may be any that keep to these rules, and one draw needn't show every extreme that they name: `cluster_ids`: in every head some of the 512 clusters receive no position.
All inputs are finite; a program needn't handle non-finite values.
Results may differ from the reference program's by a relative error of at most 0.0055.
Values may be sent and summed in bfloat16 or wider, within the bound.
No kernel may reach another device: no remote copies, remote signals or barrier semaphores. Data moves between devices by JAX's collectives and lax.ppermute only.
A program may use at most 64 MiB of HBM per device.

```python
import math
import jax
import jax.numpy as jnp
from jax import lax

D = 2048
H = 8
HD = 128
C = 512
SEQ = 4096
BATCH = 16


def draw_hidden(key, part):
    key = jax.random.fold_in(key, 5)
    key_noise, key_scale = jax.random.split(key, 2)
    values = jax.random.normal(key_noise, (BATCH, SEQ, D), jnp.float32)
    log_scale = jax.random.uniform(key_scale, (BATCH, SEQ, 1), jnp.float32, 0.0, math.log(10.0))
    return (values * jnp.exp(log_scale)).astype(jnp.bfloat16)


def draw_cluster_ids(key, part):
    key = jax.random.fold_in(key, 11)
    key_shift, key_base = jax.random.split(key, 2)
    shifts = jax.random.randint(key_shift, (H,), 0, C)
    base_ids = jax.random.randint(key_base, (BATCH, H, SEQ), 0, C - C // 16)
    return ((base_ids + shifts[None, :, None]) % C).astype(jnp.int32)


def block_levels(own_key, dims, shards, least, top_value):
    def one(axis_at, shards_of):
        heights = jax.random.uniform(jax.random.fold_in(jax.random.fold_in(own_key, 6), axis_at), (shards_of,), jnp.float32, least / len(shards), top_value / len(shards))
        return jnp.repeat(jnp.exp(heights), dims[axis_at] // shards_of).reshape((-1,) + (1,) * (len(dims) - axis_at - 1))

    loudness = one(*shards[0])
    for cut in shards[1:]:
        loudness = loudness * one(*cut)
    return loudness


def scatter_about(own_key, extent, scale, bound, pieces=(), held_as=jnp.bfloat16):
    array = jax.random.normal(own_key, extent, jnp.float32) * scale
    if len(pieces) > 0:
        array = block_levels(own_key, extent, pieces, -0.22, 0.18) * array
    return jnp.clip(array, min=-bound, max=bound).astype(held_as)


def setup_inputs(seed: int = 0) -> dict:
    key_list = jax.random.split(jax.random.key(seed), 5)
    return {
        "hidden": draw_hidden(jax.random.fold_in(key_list[4], 71), 0),
        "key_weight": scatter_about(key_list[1], (D, H * HD), D ** -0.5, 0.125, ((0, 32),)),
        "cluster_ids": draw_cluster_ids(jax.random.fold_in(key_list[4], 71), 0),
        "old_centroids": scatter_about(key_list[3], (H * C, HD), 1.0, 6.0, ((0, 512),), jnp.float32),
    }


EPSILON = 1e-06
DECAY_RATE = 0.5

def normalize_rows(values):
    return values * lax.rsqrt(lax.optimization_barrier(jnp.mean(values * values, axis=-1, keepdims=True)) + EPSILON)

def reference(hidden, key_weight, cluster_ids, old_centroids):
    flat_rows = hidden.reshape(-1, D)
    projected = jnp.dot(flat_rows, key_weight, preferred_element_type=jnp.float32).reshape(-1, H, HD)
    unit_keys = normalize_rows(projected).astype(jnp.bfloat16)
    head_keys = jnp.moveaxis(unit_keys, 1, 0)
    head_ids = jnp.moveaxis(cluster_ids, 1, 0).reshape(H, -1).astype(jnp.int32)

    def per_head(operands):
        keys_head, ids_head = operands
        sums_head = jax.ops.segment_sum(keys_head.astype(jnp.float32), ids_head, num_segments=C)
        counts_head = jax.ops.segment_sum(jnp.ones(ids_head.shape, jnp.float32), ids_head, num_segments=C)
        return (sums_head, counts_head)
    cluster_sums, cluster_counts = lax.map(per_head, (head_keys, head_ids))
    cluster_sums = cluster_sums.reshape(H * C, HD)
    cluster_counts = cluster_counts.reshape(H * C, 1)
    scaled = cluster_sums / jnp.sqrt(jnp.maximum(cluster_counts, 1.0))
    mixed = DECAY_RATE * old_centroids + (1.0 - DECAY_RATE) * scaled
    return normalize_rows(mixed)
```

```python
import jax
import jax.numpy as jnp
import numpy as np
from jax import lax
from jax.sharding import Mesh, PartitionSpec as P

EPSILON = 1e-06
DECAY_RATE = 0.5

AXES = ("z", "ylo", "core", "yhi", "x")
QUAD = ("ylo", "core")
REST = ("z", "yhi", "x")


def normalize_rows(values):
    return values * lax.rsqrt(jnp.mean(values * values, axis=-1, keepdims=True) + EPSILON)


def old_rows_permutation(quads, z_size, rows_of_quad_z):
    pairs = []
    for z in range(z_size):
        for quad in range(quads):
            source = quad * z_size + z
            pairs.append((source, z * quads + quad))
    return pairs


def per_device(hidden, key_weight, cluster_ids, old_centroids):
    z_size = lax.axis_size("z")
    quads = lax.axis_size(QUAD)
    rest = lax.axis_size(REST)
    heads = cluster_ids.shape[1]
    head_size = key_weight.shape[1] // heads
    model_width = hidden.shape[2]
    positions = hidden.shape[1]
    clusters = old_centroids.shape[0] * quads * rest // heads
    own_heads = heads // quads
    own_rows = own_heads * clusters
    block = own_rows // rest
    bf16, f32 = jnp.bfloat16, jnp.float32

    here = hidden.reshape(positions, model_width)
    swap = [(0, 1), (1, 0)]
    over_y = lax.ppermute(here, "ylo", swap)
    over_core = lax.ppermute(here, "core", swap)
    over_both = lax.ppermute(over_y, "core", swap)

    old_rows = lax.ppermute(old_centroids, ("z",) + QUAD, old_rows_permutation(quads, z_size, None))

    quad_rows = lax.all_to_all(key_weight, QUAD, split_axis=1, concat_axis=0, tiled=True)
    ids = lax.all_to_all(
        cluster_ids.reshape(quads, own_heads, positions), QUAD, split_axis=0, concat_axis=0, tiled=True
    )
    spread = jnp.broadcast_to(quad_rows[None], (z_size,) + quad_rows.shape)
    weight = lax.all_to_all(spread, "z", split_axis=0, concat_axis=0, tiled=True)
    weight = weight.reshape(model_width, own_heads * head_size)

    me = lax.axis_index(QUAD)
    flat = jnp.concatenate([here, over_core, over_y, over_both], axis=0)
    order = me ^ jnp.arange(4)
    ids = jnp.take(ids.reshape(quads, own_heads, positions), order, axis=0)
    ids = jnp.moveaxis(ids, 1, 0).reshape(own_heads, quads * positions)

    projected = jnp.dot(flat, weight, preferred_element_type=f32)
    unit_keys = normalize_rows(projected.reshape(-1, own_heads, head_size)).astype(bf16)
    cluster_iota = lax.broadcasted_iota(jnp.int32, (1, clusters, 1), 1)
    one_hot = (ids[:, None, :] == cluster_iota).astype(bf16)
    sums = jnp.einsum("hcn,nhd->hcd", one_hot, unit_keys, preferred_element_type=f32)
    counts = jnp.sum(one_hot, axis=2, dtype=f32)

    high = jnp.floor(counts * (1.0 / 32.0))
    low = counts - 32.0 * high
    sums = sums.reshape(rest, block, head_size)
    pad = [(0, 0), (0, 0), (0, head_size - block)]
    high = jnp.pad(high.reshape(rest, 1, block), pad)
    low = jnp.pad(low.reshape(rest, 1, block), pad)
    payload = jnp.concatenate(
        [sums, high, low, jnp.zeros((rest, block - 2, head_size), f32)], axis=1
    ).astype(bf16)
    arrived = lax.all_to_all(payload, REST, split_axis=0, concat_axis=0, tiled=True).astype(f32)
    total = jnp.sum(arrived, axis=0)
    share_sums = total[:block]
    share_counts = 32.0 * total[block, :block] + total[block + 1, :block]

    scaled = share_sums / jnp.sqrt(jnp.maximum(share_counts.reshape(-1, 1), 1.0))
    owned = normalize_rows(DECAY_RATE * old_rows + (1.0 - DECAY_RATE) * scaled).astype(bf16)

    spread = jnp.broadcast_to(owned[None], (rest,) + owned.shape)
    quarter = lax.all_to_all(spread, REST, split_axis=0, concat_axis=0, tiled=True)
    quarter = quarter.reshape(own_rows, head_size)
    half = lax.all_gather(quarter, "ylo", axis=0, tiled=False)
    other = lax.ppermute(half, "core", swap)
    core = lax.axis_index("core")
    first = jnp.where(core == 0, half, other)
    second = jnp.where(core == 0, other, half)
    out = jnp.stack([first, second], axis=1).astype(f32)
    return out.reshape(heads * clusters, head_size)


def solution(mesh):
    sizes = {"z": 8, "ylo": 2, "core": 2, "yhi": 4, "x": 4}
    fine = Mesh(np.asarray(mesh.devices).reshape([sizes[a] for a in AXES]), AXES)
    ctx, dp = ("z", "ylo", "core"), ("yhi", "x")
    in_specs = (P(dp, ctx, None), P(ctx, None), P(dp, None, ctx), P(ctx + dp, None))
    return jax.shard_map(
        per_device, mesh=fine, in_specs=in_specs, out_specs=P(), check_vma=False
    )
```

```python
import functools

import jax
import jax.numpy as jnp
import numpy as np
from jax import lax
from jax.experimental import pallas as pl
from jax.experimental.pallas import tpu as pltpu
from jax.sharding import Mesh, PartitionSpec as P

EPSILON = 1e-06
DECAY_RATE = 0.5

SIZES = {"z": 8, "ylo": 2, "core": 2, "yhi": 4, "xhi": 2, "xlo": 2}
AXES = tuple(SIZES)
OWNERS = ("z", "xhi")
Y = ("yhi", "ylo")
TILE = 16
COUNT_BASE = 64.0

VMEM = pl.BlockSpec(memory_space=pltpu.VMEM)
PARAMS = pltpu.CompilerParams(vmem_limit_bytes=24 * 1024 * 1024)


def old_rows_permutation():
    pairs = []
    for target, place in enumerate(np.ndindex(*SIZES.values())):
        at = dict(zip(AXES, place))
        quarter = at["core"] * SIZES["xlo"] + at["xlo"]
        owner = at["z"] * SIZES["xhi"] + at["xhi"]
        y = at["yhi"] * SIZES["ylo"] + at["ylo"]
        owners, ys = SIZES["z"] * SIZES["xhi"], SIZES["yhi"] * SIZES["ylo"]
        pairs.append(((quarter * owners + owner) * ys + y, target))
    return pairs


def split_count(counts):
    high = jnp.floor(counts * (1.0 / COUNT_BASE))
    return high, counts - COUNT_BASE * high


def sums_kernel(positions, own_heads, head_size, quarter_ref, *refs):
    pieces, weight_ref, out_ref = refs[:-2], refs[-2], refs[-1]
    owners, rows, _ = out_ref.shape
    block = rows - TILE
    clusters = owners * block // own_heads
    bf16, f32 = jnp.bfloat16, jnp.float32
    heads = pieces[0].shape[1] // (2 * positions)
    projected = [
        jnp.dot(piece[:positions, :], weight_ref[...], preferred_element_type=f32)
        for piece in pieces
    ]
    cluster = lax.broadcasted_iota(jnp.int32, (clusters, positions), 0).astype(f32)
    for head in range(own_heads):
        first = pl.multiple_of((quarter_ref[0] * own_heads + head) * positions, positions)
        second = pl.multiple_of(first + heads * positions, positions)
        sums = jnp.zeros((clusters, head_size), f32)
        counts = jnp.zeros((8, clusters), f32)
        for piece, keys in zip(pieces, projected):
            keys = keys[:, head * head_size:(head + 1) * head_size]
            mean = jnp.mean(keys * keys, axis=1, keepdims=True)
            unit_keys = (keys * lax.rsqrt(mean + EPSILON)).astype(bf16)
            high = piece[positions:, pl.ds(first, positions)].astype(f32)
            low = piece[positions:, pl.ds(second, positions)].astype(f32)
            ids = high[:1] * 32.0 + low[:1]
            one_hot = jnp.where(cluster == ids, 1.0, 0.0).astype(bf16)
            sums += jnp.dot(one_hot, unit_keys, preferred_element_type=f32)
            counts += lax.dot_general(
                jnp.ones((8, positions), bf16), one_hot, (((1,), (1,)), ((), ())),
                preferred_element_type=f32,
            )
        per_head = clusters // block
        out_ref[head * per_head:(head + 1) * per_head, :block, :] = sums.reshape(
            per_head, block, head_size
        ).astype(bf16)
        row = lax.broadcasted_iota(jnp.int32, (TILE, block), 0)
        for part in range(per_head):
            high, low = split_count(counts[:1, part * block:(part + 1) * block])
            lines = jnp.where(row == 0, high, jnp.where(row == 1, low, 0.0))
            lines = jnp.concatenate([lines, jnp.zeros((TILE, head_size - block), f32)], axis=1)
            out_ref[head * per_head + part, block:, :] = lines.astype(bf16)


def share_kernel(arrived_ref, old_ref, out_ref):
    block = arrived_ref.shape[1] - TILE
    bf16, f32 = jnp.bfloat16, jnp.float32
    total = arrived_ref[0].astype(f32)
    for source in range(1, arrived_ref.shape[0]):
        total += arrived_ref[source].astype(f32)
    counts = total[block:block + 1] * COUNT_BASE + total[block + 1:block + 2]
    high, low = split_count(counts)
    row = lax.broadcasted_iota(jnp.int32, (TILE, total.shape[1]), 0)
    lines = jnp.where(row == 0, high, jnp.where(row == 1, low, 0.0))
    old_high = old_ref[...].astype(bf16).astype(f32)
    old = jnp.concatenate([old_high, old_ref[...] - old_high], axis=0)
    for target in range(out_ref.shape[0]):
        out_ref[target, :block, :] = total[:block].astype(bf16)
        out_ref[target, block:block + TILE, :] = lines.astype(bf16)
        out_ref[target, block + TILE:, :] = old.astype(bf16)


def update_kernel(arrived_ref, out_ref):
    sources = arrived_ref.shape[0]
    block = out_ref.shape[1]
    f32 = jnp.float32
    total = arrived_ref[0, :block + TILE, :].astype(f32)
    for source in range(1, sources):
        total += arrived_ref[source, :block + TILE, :].astype(f32)
    counts = total[block:block + 1, :block] * COUNT_BASE + total[block + 1:block + 2, :block]
    diagonal = lax.broadcasted_iota(jnp.int32, (block, block), 0) == lax.broadcasted_iota(
        jnp.int32, (block, block), 1
    )
    counts = jnp.sum(jnp.where(diagonal, counts, 0.0), axis=1, keepdims=True)
    old = []
    for source in range(sources):
        both = arrived_ref[source, block + TILE:, :].astype(f32)
        old.append(both[:TILE // 2] + both[TILE // 2:])
    old = jnp.concatenate(old, axis=0)
    scaled = total[:block] / jnp.sqrt(jnp.maximum(counts, 1.0))
    mixed = DECAY_RATE * old + (1.0 - DECAY_RATE) * scaled
    mean = jnp.mean(mixed * mixed, axis=1, keepdims=True)
    centroids = (mixed * lax.rsqrt(mean + EPSILON)).astype(jnp.bfloat16)
    for target in range(out_ref.shape[0]):
        out_ref[target] = centroids


def per_device(hidden, key_weight, cluster_ids, old_centroids):
    _, positions, model_width = hidden.shape
    heads = cluster_ids.shape[1]
    head_size = key_weight.shape[1] // heads
    cores, xlos = SIZES["core"], SIZES["xlo"]
    quads, owners, ys = cores * xlos, SIZES["z"] * SIZES["xhi"], SIZES["yhi"] * SIZES["ylo"]
    own_heads = heads // quads
    columns = own_heads * head_size
    block = old_centroids.shape[0] * ys
    clusters = block * owners // own_heads
    bf16, f32 = jnp.bfloat16, jnp.float32
    core, xlo = lax.axis_index("core"), lax.axis_index("xlo")
    quarter = core * xlos + xlo

    mine = key_weight.reshape(-1, cores, xlos, columns)
    mine = lax.dynamic_index_in_dim(mine, xlo, axis=2, keepdims=False)
    mine = lax.all_to_all(jnp.moveaxis(mine, 1, 0), "core", split_axis=0, concat_axis=0, tiled=True)
    mine = mine.reshape(1, -1, columns)
    spread = jnp.broadcast_to(mine, (SIZES["z"] * SIZES["ylo"],) + mine.shape[1:])
    weight = lax.all_to_all(spread, ("z", "ylo"), split_axis=0, concat_axis=0, tiled=True)
    weight = weight.reshape(model_width, columns)

    ids = cluster_ids.reshape(1, heads * positions)
    ids = jnp.concatenate([ids >> 5, ids & 31], axis=1).astype(bf16)
    here = jnp.concatenate(
        [hidden.reshape(positions, model_width), ids, jnp.zeros((TILE - 1, model_width), bf16)], axis=0
    )
    swap = [(0, 1), (1, 0)]
    over_x = lax.ppermute(here, "xlo", swap)
    over_core = lax.ppermute(here, "core", swap)
    over_both = lax.ppermute(over_x, "core", swap)
    old_rows = lax.ppermute(old_centroids, AXES, old_rows_permutation())

    payload = pl.pallas_call(
        functools.partial(sums_kernel, positions, own_heads, head_size),
        out_shape=jax.ShapeDtypeStruct((owners, block + TILE, head_size), bf16),
        in_specs=[pl.BlockSpec(memory_space=pltpu.SMEM)] + [VMEM] * 5,
        out_specs=VMEM,
        compiler_params=PARAMS,
        cost_estimate=pl.CostEstimate(flops=10**9, bytes_accessed=4 * 10**6, transcendentals=0),
    )(quarter.reshape(1), here, over_core, over_x, over_both, weight)
    arrived = lax.all_to_all(payload, OWNERS, split_axis=0, concat_axis=0, tiled=True)

    shares = pl.pallas_call(
        share_kernel,
        out_shape=jax.ShapeDtypeStruct((ys, block + 2 * TILE, head_size), bf16),
        in_specs=[VMEM, VMEM],
        out_specs=VMEM,
        compiler_params=PARAMS,
    )(arrived, old_rows)
    arrived = lax.all_to_all(shares, Y, split_axis=0, concat_axis=0, tiled=True)

    owned = pl.pallas_call(
        update_kernel,
        out_shape=jax.ShapeDtypeStruct((xlos * owners, block, head_size), bf16),
        in_specs=[VMEM],
        out_specs=VMEM,
        compiler_params=PARAMS,
    )(arrived)
    half = lax.all_to_all(owned, ("xlo",) + OWNERS, split_axis=0, concat_axis=0, tiled=True)
    half = half.reshape(-1, head_size)
    other = lax.ppermute(half, "core", swap)
    first = jnp.where(core == 0, half, other)
    second = jnp.where(core == 0, other, half)
    return jnp.concatenate([first, second], axis=0).astype(f32)


def solution(mesh):
    fine = Mesh(np.asarray(mesh.devices).reshape(tuple(SIZES.values())), AXES)
    ctx, dp = ("z", "ylo", "core"), ("yhi", "xhi", "xlo")
    in_specs = (P(dp, ctx, None), P(ctx, None), P(dp, None, ctx), P(ctx + dp, None))
    return jax.shard_map(
        per_device, mesh=fine, in_specs=in_specs, out_specs=P(), check_vma=False
    )
```

```python
import functools

import jax
import jax.numpy as jnp
import numpy as np
from jax import lax
from jax.experimental import pallas as pl
from jax.experimental.pallas import tpu as pltpu
from jax.sharding import Mesh, PartitionSpec as P

EPSILON = 1e-06
DECAY_RATE = 0.5

SIZES = {"z": 8, "ylo": 2, "core": 2, "yhi": 4, "x": 4}
AXES = tuple(SIZES)
RING = ("core", "x")
Y = ("yhi", "ylo")
TILE = 16
COUNT_BASE = 64.0
OLD_AT = 8

VMEM = pl.BlockSpec(memory_space=pltpu.VMEM)
ANY = pl.BlockSpec(memory_space=pl.ANY)
ALONE = pltpu.CompilerParams(vmem_limit_bytes=56 * 1024 * 1024)
PARAMS = pltpu.CompilerParams(vmem_limit_bytes=24 * 1024 * 1024)


def turn(step):
    xs = SIZES["x"]
    return [
        (core * xs + x, core * xs + (x + (step if core == 0 else -step)) % xs)
        for core in range(SIZES["core"])
        for x in range(xs)
    ]


def place_of(ids):
    ylo, core = ids >> 8, (ids >> 7) & 1
    yhi, x, row = (ids >> 5) & 3, (ids >> 3) & 3, ids & 7
    return (core * 4 + x) * 64 + (yhi * 2 + ylo) * 8 + row


def block_of(z, y):
    core, x, yhi, ylo = z // 4, z % 4, y // 2, y % 2
    return ylo * 32 + core * 16 + yhi * 4 + x


def count_lines(counts, rest):
    high = jnp.floor(counts * (1.0 / COUNT_BASE))
    low = counts - COUNT_BASE * high
    row = lax.broadcasted_iota(jnp.int32, rest.shape, 0)
    return jnp.where(row == 0, high, jnp.where(row == 1, low, jnp.where(row < OLD_AT, 0.0, rest)))


def join_kernel(
    hidden_ref, ids_ref, old_ref, weight_ref, out_ref, spread_ref,
    ids_held, old_held, held, weight_held, spread_held, sems,
):
    positions = hidden_ref.shape[0]
    targets, cores, _, head_size = spread_ref.shape
    bf16, f32 = jnp.bfloat16, jnp.float32
    xs = weight_ref.shape[1] // (cores * head_size)
    x = lax.axis_index("x")
    moves = [
        pltpu.make_async_copy(ids_ref, ids_held, sems.at[0]),
        pltpu.make_async_copy(old_ref, old_held, sems.at[1]),
        pltpu.make_async_copy(weight_ref, weight_held, sems.at[2]),
        pltpu.make_async_copy(hidden_ref, held.at[pl.ds(0, positions)], sems.at[3]),
    ]
    for move in moves:
        move.start()
    moves[0].wait()
    moves[1].wait()
    place = place_of(ids_held[...])
    heads, width = place.shape
    parts = ((place >> 5).astype(f32), (place & 31).astype(f32))
    row = lax.broadcasted_iota(jnp.int32, (OLD_AT, width), 0)
    old = old_held[...]
    for number in range(2 * heads):
        part, head = divmod(number, heads)
        line = jnp.where(row == 0, parts[part][head:head + 1], 0.0)
        rest = old if number == 0 else jnp.zeros_like(old)
        lines = jnp.concatenate([line, rest], axis=0).astype(bf16)
        held[positions:, number * width:(number + 1) * width] = lines
    moves[3].wait()
    out = pltpu.make_async_copy(held, out_ref, sems.at[4])
    out.start()
    moves[2].wait()
    for core in range(cores):
        first = pl.multiple_of((core * xs + x) * head_size, head_size)
        columns = weight_held[:, pl.ds(first, head_size)]
        for target in range(targets):
            spread_held[target, core] = columns
    spread = pltpu.make_async_copy(spread_held, spread_ref, sems.at[5])
    spread.start()
    out.wait()
    spread.wait()


def sums_kernel(positions, *refs):
    pieces = refs[:8]
    mine_ref, others_ref, out_ref, held, mine_held, others_held, weight, old_ref, sems = refs[8:]
    owners, rows, head_size = out_ref.shape
    block = rows - TILE
    clusters = owners * block
    xs = owners // 2
    bf16, f32 = jnp.bfloat16, jnp.float32
    core, x, z = lax.axis_index("core"), lax.axis_index("x"), lax.axis_index("z")
    moves = [
        pltpu.make_async_copy(mine_ref, mine_held, sems.at[0]),
        pltpu.make_async_copy(others_ref, others_held, sems.at[1]),
    ]
    moves += [
        pltpu.make_async_copy(piece, held.at[number], sems.at[2 + number])
        for number, piece in enumerate(pieces)
    ]
    for move in moves:
        move.start()
    head = core * xs + x
    heads = held.shape[2] // (2 * positions)
    first = pl.multiple_of(head * positions, positions)
    second = pl.multiple_of(first + heads * positions, positions)
    cluster = lax.broadcasted_iota(jnp.int32, (clusters, positions), 0).astype(f32)
    mine = (head == z).astype(f32)
    moves[0].wait()
    moves[1].wait()
    for source in range(mine_held.shape[0]):
        weight[source, core] = mine_held[source, core]
        weight[source, 1 - core] = others_held[source, core]
    whole = weight[...].reshape(held.shape[2], head_size)
    keys, hots = [], []
    for number in range(len(pieces)):
        moves[2 + number].wait()
        key = jnp.dot(held[number, :positions, :], whole, preferred_element_type=f32)
        mean = jnp.mean(key * key, axis=1, keepdims=True)
        keys.append((key * lax.rsqrt(mean + EPSILON)).astype(bf16))
        high = held[number, positions:, pl.ds(first, positions)].astype(f32)
        low = held[number, positions:, pl.ds(second, positions)].astype(f32)
        ids = high[:1] * 32.0 + low[:1]
        hots.append(jnp.where(cluster == ids, 1.0, 0.0).astype(bf16))
        other, kind = divmod(number, xs)
        source = 1 - core if other else core
        sign = 2 * source - 1
        moved = (x + (0, sign, -sign, 2)[kind] + xs) % xs
        old_ref[source * xs + moved] = held[number, positions:, :head_size].astype(f32) * mine
    one_hot, unit_keys = jnp.concatenate(hots, axis=1), jnp.concatenate(keys, axis=0)
    sums = jnp.dot(one_hot, unit_keys, preferred_element_type=f32)
    counts = lax.dot_general(
        jnp.ones((8, one_hot.shape[1]), bf16), one_hot, (((1,), (1,)), ((), ())),
        preferred_element_type=f32,
    )[:1]
    empty = jnp.zeros((1, head_size - block), f32)
    for owner in range(owners):
        own = slice(owner * block, (owner + 1) * block)
        out_ref[owner, :block, :] = sums[own].astype(bf16)
        padded = jnp.concatenate([counts[:, own], empty], axis=1)
        out_ref[owner, block:, :] = count_lines(padded, old_ref[owner]).astype(bf16)


def share_kernel(arrived_ref, out_ref):
    block = arrived_ref.shape[1] - TILE
    bf16, f32 = jnp.bfloat16, jnp.float32
    total = arrived_ref[0].astype(f32)
    for source in range(1, arrived_ref.shape[0]):
        total += arrived_ref[source].astype(f32)
    counts = total[block:block + 1] * COUNT_BASE + total[block + 1:block + 2]
    sums = total[:block].astype(bf16)
    lines = count_lines(counts, total[block:]).astype(bf16)
    for target in range(out_ref.shape[0]):
        out_ref[target, :block, :] = sums
        out_ref[target, block:, :] = lines


def update_kernel(arrived_ref, out_ref):
    sources = arrived_ref.shape[0]
    block = out_ref.shape[1]
    f32 = jnp.float32
    total = arrived_ref[0].astype(f32)
    old = [total[block + OLD_AT:]]
    for source in range(1, sources):
        arrived = arrived_ref[source].astype(f32)
        old.append(arrived[block + OLD_AT:])
        total += arrived
    old = jnp.concatenate(old, axis=0)
    counts = total[block:block + 1, :block] * COUNT_BASE + total[block + 1:block + 2, :block]
    diagonal = lax.broadcasted_iota(jnp.int32, (block, block), 0) == lax.broadcasted_iota(
        jnp.int32, (block, block), 1
    )
    counts = jnp.sum(jnp.where(diagonal, counts, 0.0), axis=1, keepdims=True)
    scaled = total[:block] / jnp.sqrt(jnp.maximum(counts, 1.0))
    mixed = DECAY_RATE * old + (1.0 - DECAY_RATE) * scaled
    mean = jnp.mean(mixed * mixed, axis=1, keepdims=True)
    centroids = (mixed * lax.rsqrt(mean + EPSILON)).astype(jnp.bfloat16)
    for target in range(out_ref.shape[0]):
        out_ref[target] = centroids


def rows_kernel(mine_ref, other_ref, out_ref, held, rows_held, in_sems, out_sems):
    core = lax.axis_index("core")
    cores, xs, owners, block, _ = held.shape
    moves = []
    for number, ref in enumerate((mine_ref, other_ref)):
        for x in range(xs):
            moves.append(pltpu.make_async_copy(
                ref.at[x], held.at[number, x], in_sems.at[number * xs + x]
            ))
    for move in moves:
        move.start()
    lasts = []
    for number, place in enumerate((core, 1 - core)):
        for x in range(xs):
            moves[number * xs + x].wait()
            for z in range(owners):
                rows = held[number, x, z].astype(jnp.float32)
                for y in range(block // 8):
                    at = block_of(z, y) * 8
                    rows_held[number, x, at:at + 8, :] = rows[y * 8:(y + 1) * 8]
            last = pltpu.make_async_copy(
                rows_held.at[number, x], out_ref.at[place, x], out_sems.at[number * xs + x]
            )
            last.start()
            lasts.append(last)
    for last in lasts:
        last.wait()


def per_device(hidden, key_weight, cluster_ids, old_centroids):
    _, positions, model_width = hidden.shape
    heads = cluster_ids.shape[1]
    head_size = key_weight.shape[1] // heads
    cores, xs, zs = SIZES["core"], SIZES["x"], SIZES["z"]
    ylos = SIZES["ylo"]
    ys = SIZES["yhi"] * ylos
    block = old_centroids.shape[0] * ys
    clusters = block * zs
    bf16, f32 = jnp.bfloat16, jnp.float32

    here, spread = pl.pallas_call(
        join_kernel,
        out_shape=(
            jax.ShapeDtypeStruct((positions + TILE, model_width), bf16),
            jax.ShapeDtypeStruct((zs * ylos, cores, key_weight.shape[0], head_size), bf16),
        ),
        in_specs=[ANY] * 4,
        out_specs=(ANY, ANY),
        scratch_shapes=[
            pltpu.VMEM((heads, positions), jnp.int32),
            pltpu.VMEM(old_centroids.shape, f32),
            pltpu.VMEM((positions + TILE, model_width), bf16),
            pltpu.VMEM(key_weight.shape, bf16),
            pltpu.VMEM((zs * ylos, cores, key_weight.shape[0], head_size), bf16),
            pltpu.SemaphoreType.DMA((6,)),
        ],
        compiler_params=ALONE,
    )(
        hidden.reshape(positions, model_width), cluster_ids.reshape(heads, positions),
        old_centroids, key_weight,
    )
    swap = [(0, 1), (1, 0)]
    up = lax.ppermute(here, RING, turn(1))
    down = lax.ppermute(here, RING, turn(-1))
    weight = lax.all_to_all(spread, ("z", "ylo"), split_axis=0, concat_axis=0, tiled=True)
    others = lax.ppermute(weight, "core", swap)
    far = lax.ppermute(up, RING, turn(1))
    pieces = [here, up, down, far]
    pieces += [lax.ppermute(piece, "core", swap) for piece in pieces]

    payload = pl.pallas_call(
        functools.partial(sums_kernel, positions),
        out_shape=jax.ShapeDtypeStruct((zs, block + TILE, head_size), bf16),
        in_specs=[ANY] * (len(pieces) + 2),
        out_specs=VMEM,
        scratch_shapes=[
            pltpu.VMEM((len(pieces),) + here.shape, bf16),
            pltpu.VMEM(weight.shape, bf16),
            pltpu.VMEM(weight.shape, bf16),
            pltpu.VMEM(weight.shape, bf16),
            pltpu.VMEM((zs, TILE, head_size), f32),
            pltpu.SemaphoreType.DMA((len(pieces) + 2,)),
        ],
        compiler_params=ALONE,
        cost_estimate=pl.CostEstimate(flops=10**9, bytes_accessed=6 * 10**6, transcendentals=0),
    )(*pieces, weight, others)
    arrived = lax.all_to_all(payload, "z", split_axis=0, concat_axis=0, tiled=True)

    shares = pl.pallas_call(
        share_kernel,
        out_shape=jax.ShapeDtypeStruct((ys, block + TILE, head_size), bf16),
        in_specs=[VMEM],
        out_specs=VMEM,
        compiler_params=PARAMS,
    )(arrived)
    arrived = lax.all_to_all(shares, Y, split_axis=0, concat_axis=0, tiled=True)

    owned = pl.pallas_call(
        update_kernel,
        out_shape=jax.ShapeDtypeStruct((xs * zs, block, head_size), bf16),
        in_specs=[VMEM],
        out_specs=VMEM,
        compiler_params=PARAMS,
    )(arrived)
    half = lax.all_to_all(owned, ("x", "z"), split_axis=0, concat_axis=0, tiled=True)
    half = half.reshape(xs, zs, block, head_size)
    other = lax.ppermute(half, "core", swap)
    out = pl.pallas_call(
        rows_kernel,
        out_shape=jax.ShapeDtypeStruct((cores, xs, clusters, head_size), f32),
        in_specs=[ANY, ANY],
        out_specs=ANY,
        scratch_shapes=[
            pltpu.VMEM((cores,) + half.shape, bf16),
            pltpu.VMEM((cores, xs, clusters, head_size), f32),
            pltpu.SemaphoreType.DMA((cores * xs,)),
            pltpu.SemaphoreType.DMA((cores * xs,)),
        ],
        compiler_params=ALONE,
    )(half, other)
    return out.reshape(heads * clusters, head_size)


def solution(mesh):
    fine = Mesh(np.asarray(mesh.devices).reshape(tuple(SIZES.values())), AXES)
    ctx, dp = ("z", "ylo", "core"), ("yhi", "x")
    in_specs = (P(dp, ctx, None), P(ctx, None), P(dp, None, ctx), P(ctx + dp, None))
    return jax.shard_map(
        per_device, mesh=fine, in_specs=in_specs, out_specs=P(), check_vma=False
    )
```

```python
import functools

import jax
import jax.numpy as jnp
import numpy as np
from jax import lax
from jax.experimental import pallas as pl
from jax.experimental.pallas import tpu as pltpu
from jax.sharding import Mesh, PartitionSpec as P

EPSILON = 1e-06
DECAY_RATE = 0.5

SIZES = {"z": 8, "ylo": 2, "core": 2, "yhi": 4, "x": 4}
AXES = tuple(SIZES)
RING = ("core", "x")
Y = ("yhi", "ylo")
TILE = 16
COUNT_BASE = 64.0
OLD_AT = 8

VMEM = pl.BlockSpec(memory_space=pltpu.VMEM)
ANY = pl.BlockSpec(memory_space=pl.ANY)
ALONE = pltpu.CompilerParams(vmem_limit_bytes=63_200_000)
PARAMS = pltpu.CompilerParams(vmem_limit_bytes=24 * 1024 * 1024)


def turn(step):
    xs = SIZES["x"]
    return [
        (core * xs + x, core * xs + (x + (step if core == 0 else -step)) % xs)
        for core in range(SIZES["core"])
        for x in range(xs)
    ]


def place_of(ids):
    ylo, core = ids >> 8, (ids >> 7) & 1
    yhi, x, row = (ids >> 5) & 3, (ids >> 3) & 3, ids & 7
    return (core * 4 + x) * 64 + (yhi * 2 + ylo) * 8 + row


def block_of(z, y):
    core, x, yhi, ylo = z // 4, z % 4, y // 2, y % 2
    return ylo * 32 + core * 16 + yhi * 4 + x


def count_lines(counts, rest):
    high = jnp.floor(counts * (1.0 / COUNT_BASE))
    low = counts - COUNT_BASE * high
    row = lax.broadcasted_iota(jnp.int32, rest.shape, 0)
    return jnp.where(row == 0, high, jnp.where(row == 1, low, jnp.where(row < OLD_AT, 0.0, rest)))


def join_kernel(
    hidden_ref, ids_ref, old_ref, weight_ref, out_ref, spread_ref,
    ids_held, old_held, held, weight_held, spread_held, sems,
):
    positions = hidden_ref.shape[0]
    targets, cores, _, head_size = spread_ref.shape
    bf16, f32 = jnp.bfloat16, jnp.float32
    xs = weight_ref.shape[1] // (cores * head_size)
    x = lax.axis_index("x")
    moves = [
        pltpu.make_async_copy(ids_ref, ids_held, sems.at[0]),
        pltpu.make_async_copy(old_ref, old_held, sems.at[1]),
        pltpu.make_async_copy(weight_ref, weight_held, sems.at[2]),
        pltpu.make_async_copy(hidden_ref, held.at[pl.ds(0, positions)], sems.at[3]),
    ]
    for move in moves:
        move.start()
    moves[0].wait()
    moves[1].wait()
    place = place_of(ids_held[...])
    heads, width = place.shape
    parts = ((place >> 5).astype(f32), (place & 31).astype(f32))
    row = lax.broadcasted_iota(jnp.int32, (OLD_AT, width), 0)
    old = old_held[...]
    for number in range(2 * heads):
        part, head = divmod(number, heads)
        line = jnp.where(row == 0, parts[part][head:head + 1], 0.0)
        rest = old if number == 0 else jnp.zeros_like(old)
        lines = jnp.concatenate([line, rest], axis=0).astype(bf16)
        held[positions:, number * width:(number + 1) * width] = lines
    moves[3].wait()
    out = pltpu.make_async_copy(held, out_ref, sems.at[4])
    out.start()
    moves[2].wait()
    for core in range(cores):
        first = pl.multiple_of((core * xs + x) * head_size, head_size)
        columns = weight_held[:, pl.ds(first, head_size)]
        for target in range(targets):
            spread_held[target, core] = columns
    spread = pltpu.make_async_copy(spread_held, spread_ref, sems.at[5])
    spread.start()
    out.wait()
    spread.wait()


def sums_kernel(positions, *refs):
    pieces = refs[:8]
    mine_ref, others_ref, out_ref, weight, old_ref = refs[8:]
    owners, rows, head_size = out_ref.shape
    block = rows - TILE
    clusters = owners * block
    xs = owners // 2
    bf16, f32 = jnp.bfloat16, jnp.float32
    core, x, z = lax.axis_index("core"), lax.axis_index("x"), lax.axis_index("z")
    head = core * xs + x
    model_width = pieces[0].shape[1]
    heads = model_width // (2 * positions)
    first = pl.multiple_of(head * positions, positions)
    second = pl.multiple_of(first + heads * positions, positions)
    cluster = lax.broadcasted_iota(jnp.int32, (clusters, positions), 0).astype(f32)
    mine = (head == z).astype(f32)
    @pl.when(core == 0)
    def _():
        weight[:, 0] = mine_ref[:, 0]
        weight[:, 1] = others_ref[:, 0]

    @pl.when(core == 1)
    def _():
        weight[:, 1] = mine_ref[:, 1]
        weight[:, 0] = others_ref[:, 1]

    whole = weight[...].reshape(model_width, head_size)
    keys, hots = [], []
    for number, piece in enumerate(pieces):
        key = jnp.dot(piece[:positions, :], whole, preferred_element_type=f32)
        mean = jnp.mean(key * key, axis=1, keepdims=True)
        keys.append((key * lax.rsqrt(mean + EPSILON)).astype(bf16))
        high = piece[positions:, pl.ds(first, positions)].astype(f32)
        low = piece[positions:, pl.ds(second, positions)].astype(f32)
        ids = high[:1] * 32.0 + low[:1]
        hots.append(jnp.where(cluster == ids, 1.0, 0.0).astype(bf16))
        other, kind = divmod(number, xs)
        source = 1 - core if other else core
        sign = 2 * source - 1
        moved = (x + (0, sign, -sign, 2)[kind] + xs) % xs
        old_ref[source * xs + moved] = piece[positions:, :head_size].astype(f32) * mine
    one_hot, unit_keys = jnp.concatenate(hots, axis=1), jnp.concatenate(keys, axis=0)
    sums = jnp.dot(one_hot, unit_keys, preferred_element_type=f32)
    counts = lax.dot_general(
        jnp.ones((8, one_hot.shape[1]), bf16), one_hot, (((1,), (1,)), ((), ())),
        preferred_element_type=f32,
    )[:1]
    empty = jnp.zeros((1, head_size - block), f32)
    for owner in range(owners):
        own = slice(owner * block, (owner + 1) * block)
        out_ref[owner, :block, :] = sums[own].astype(bf16)
        padded = jnp.concatenate([counts[:, own], empty], axis=1)
        out_ref[owner, block:, :] = count_lines(padded, old_ref[owner]).astype(bf16)


def share_kernel(arrived_ref, out_ref):
    block = arrived_ref.shape[1] - TILE
    bf16, f32 = jnp.bfloat16, jnp.float32
    total = arrived_ref[0].astype(f32)
    for source in range(1, arrived_ref.shape[0]):
        total += arrived_ref[source].astype(f32)
    counts = total[block:block + 1] * COUNT_BASE + total[block + 1:block + 2]
    sums = total[:block].astype(bf16)
    lines = count_lines(counts, total[block:]).astype(bf16)
    for target in range(out_ref.shape[0]):
        out_ref[target, :block, :] = sums
        out_ref[target, block:, :] = lines


def update_kernel(arrived_ref, out_ref):
    sources = arrived_ref.shape[0]
    block = out_ref.shape[1]
    f32 = jnp.float32
    total = arrived_ref[0].astype(f32)
    old = [total[block + OLD_AT:]]
    for source in range(1, sources):
        arrived = arrived_ref[source].astype(f32)
        old.append(arrived[block + OLD_AT:])
        total += arrived
    old = jnp.concatenate(old, axis=0)
    counts = total[block:block + 1, :block] * COUNT_BASE + total[block + 1:block + 2, :block]
    diagonal = lax.broadcasted_iota(jnp.int32, (block, block), 0) == lax.broadcasted_iota(
        jnp.int32, (block, block), 1
    )
    counts = jnp.sum(jnp.where(diagonal, counts, 0.0), axis=1, keepdims=True)
    scaled = total[:block] / jnp.sqrt(jnp.maximum(counts, 1.0))
    mixed = DECAY_RATE * old + (1.0 - DECAY_RATE) * scaled
    mean = jnp.mean(mixed * mixed, axis=1, keepdims=True)
    centroids = (mixed * lax.rsqrt(mean + EPSILON)).astype(jnp.bfloat16)
    for target in range(out_ref.shape[0]):
        out_ref[target] = centroids


def per_device(hidden, key_weight, cluster_ids, old_centroids):
    _, positions, model_width = hidden.shape
    heads = cluster_ids.shape[1]
    head_size = key_weight.shape[1] // heads
    cores, xs, zs = SIZES["core"], SIZES["x"], SIZES["z"]
    ylos = SIZES["ylo"]
    ys = SIZES["yhi"] * ylos
    block = old_centroids.shape[0] * ys
    clusters = block * zs
    bf16, f32 = jnp.bfloat16, jnp.float32

    core = lax.axis_index("core")
    here, spread = pl.pallas_call(
        join_kernel,
        out_shape=(
            jax.ShapeDtypeStruct((positions + TILE, model_width), bf16),
            jax.ShapeDtypeStruct((zs * ylos, cores, key_weight.shape[0], head_size), bf16),
        ),
        in_specs=[ANY] * 4,
        out_specs=(ANY, ANY),
        scratch_shapes=[
            pltpu.VMEM((heads, positions), jnp.int32),
            pltpu.VMEM(old_centroids.shape, f32),
            pltpu.VMEM((positions + TILE, model_width), bf16),
            pltpu.VMEM(key_weight.shape, bf16),
            pltpu.VMEM((zs * ylos, cores, key_weight.shape[0], head_size), bf16),
            pltpu.SemaphoreType.DMA((6,)),
        ],
        compiler_params=ALONE,
    )(
        hidden.reshape(positions, model_width), cluster_ids.reshape(heads, positions),
        old_centroids, key_weight,
    )
    swap = [(0, 1), (1, 0)]
    up = lax.ppermute(here, RING, turn(1))
    down = lax.ppermute(here, RING, turn(-1))
    weight = lax.all_to_all(spread, ("z", "ylo"), split_axis=0, concat_axis=0, tiled=True)
    others = lax.ppermute(weight, "core", swap)
    up, down, here_too = lax.optimization_barrier((up, down, here))
    far = lax.ppermute(up, RING, turn(1))
    pieces = [here, up, down, far]
    pieces += [lax.ppermute(piece, "core", swap) for piece in (here_too, up, down, far)]

    payload = pl.pallas_call(
        functools.partial(sums_kernel, positions),
        out_shape=jax.ShapeDtypeStruct((zs, block + TILE, head_size), bf16),
        in_specs=[VMEM] * (len(pieces) + 2),
        out_specs=VMEM,
        scratch_shapes=[
            pltpu.VMEM(weight.shape, bf16),
            pltpu.VMEM((zs, TILE, head_size), f32),
        ],
        compiler_params=PARAMS,
        cost_estimate=pl.CostEstimate(flops=10**9, bytes_accessed=6 * 10**6, transcendentals=0),
    )(*pieces, weight, others)
    arrived = lax.all_to_all(payload, "z", split_axis=0, concat_axis=0, tiled=True)

    shares = pl.pallas_call(
        share_kernel,
        out_shape=jax.ShapeDtypeStruct((ys, block + TILE, head_size), bf16),
        in_specs=[VMEM],
        out_specs=VMEM,
        compiler_params=PARAMS,
    )(arrived)
    arrived = lax.all_to_all(shares, Y, split_axis=0, concat_axis=0, tiled=True)

    owned = pl.pallas_call(
        update_kernel,
        out_shape=jax.ShapeDtypeStruct((xs * zs, block, head_size), bf16),
        in_specs=[VMEM],
        out_specs=VMEM,
        compiler_params=PARAMS,
    )(arrived)
    half = lax.all_to_all(owned, ("x", "z"), split_axis=0, concat_axis=0, tiled=True)
    half = half.reshape(xs, zs, block, head_size)
    other = lax.ppermute(half, "core", swap)
    first = jnp.where(core == 0, half, other)
    second = jnp.where(core == 0, other, half)
    out = jnp.stack([first, second]).reshape(cores, xs, cores, xs, SIZES["yhi"], ylos, 8, head_size)
    out = jnp.transpose(out, (0, 1, 5, 2, 4, 3, 6, 7)).astype(f32)
    return out.reshape(heads * clusters, head_size)


def solution(mesh):
    fine = Mesh(np.asarray(mesh.devices).reshape(tuple(SIZES.values())), AXES)
    ctx, dp = ("z", "ylo", "core"), ("yhi", "x")
    in_specs = (P(dp, ctx, None), P(ctx, None), P(dp, None, ctx), P(ctx + dp, None))
    return jax.shard_map(
        per_device, mesh=fine, in_specs=in_specs, out_specs=P(), check_vma=False
    )
```

```python
import functools

import jax
import jax.numpy as jnp
import numpy as np
from jax import lax
from jax.experimental import pallas as pl
from jax.experimental.pallas import tpu as pltpu
from jax.sharding import Mesh, PartitionSpec as P

EPSILON = 1e-06
DECAY_RATE = 0.5

SIZES = {"z": 8, "ylo": 2, "core": 2, "yhi": 4, "x": 4}
AXES = tuple(SIZES)
RING = ("core", "x")
Y = ("yhi", "ylo")
TILE = 16
COUNT_BASE = 64.0
OLD_AT = 8
CLUSTERS = 512

VMEM = pl.BlockSpec(memory_space=pltpu.VMEM)
ANY = pl.BlockSpec(memory_space=pl.ANY)
ALONE = pltpu.CompilerParams(vmem_limit_bytes=63_200_000)
PARAMS = pltpu.CompilerParams(vmem_limit_bytes=24 * 1024 * 1024)


def turn(step):
    xs = SIZES["x"]
    return [
        (core * xs + x, core * xs + (x + (step if core == 0 else -step)) % xs)
        for core in range(SIZES["core"])
        for x in range(xs)
    ]


def place_of(ids):
    ylo, core = ids >> 8, (ids >> 7) & 1
    yhi, x, row = (ids >> 5) & 3, (ids >> 3) & 3, ids & 7
    return (core * 4 + x) * 64 + (yhi * 2 + ylo) * 8 + row


def block_of(z, y):
    core, x, yhi, ylo = z // 4, z % 4, y // 2, y % 2
    return ylo * 32 + core * 16 + yhi * 4 + x


def count_lines(counts, rest):
    high = jnp.floor(counts * (1.0 / COUNT_BASE))
    low = counts - COUNT_BASE * high
    row = lax.broadcasted_iota(jnp.int32, rest.shape, 0)
    return jnp.where(row == 0, high, jnp.where(row == 1, low, jnp.where(row < OLD_AT, 0.0, rest)))


def join_kernel(
    hidden_ref, ids_ref, old_ref, weight_ref, out_ref, spread_ref,
    ids_held, old_held, held, weight_held, spread_held, sems,
):
    positions = hidden_ref.shape[0]
    targets, cores, _, head_size = spread_ref.shape
    bf16, f32 = jnp.bfloat16, jnp.float32
    xs = weight_ref.shape[1] // (cores * head_size)
    x = lax.axis_index("x")
    moves = [
        pltpu.make_async_copy(ids_ref, ids_held, sems.at[0]),
        pltpu.make_async_copy(old_ref, old_held, sems.at[1]),
        pltpu.make_async_copy(weight_ref, weight_held, sems.at[2]),
        pltpu.make_async_copy(hidden_ref, held.at[pl.ds(0, positions)], sems.at[3]),
    ]
    for move in moves:
        move.start()
    moves[0].wait()
    moves[1].wait()
    place = place_of(ids_held[...])
    heads, width = place.shape
    parts = ((place >> 5).astype(f32), (place & 31).astype(f32))
    row = lax.broadcasted_iota(jnp.int32, (OLD_AT, width), 0)
    old = old_held[...]
    for number in range(2 * heads):
        part, head = divmod(number, heads)
        line = jnp.where(row == 0, parts[part][head:head + 1], 0.0)
        rest = old if number == 0 else jnp.zeros_like(old)
        lines = jnp.concatenate([line, rest], axis=0).astype(bf16)
        held[positions:, number * width:(number + 1) * width] = lines
    moves[3].wait()
    out = pltpu.make_async_copy(held, out_ref, sems.at[4])
    out.start()
    moves[2].wait()
    for core in range(cores):
        first = pl.multiple_of((core * xs + x) * head_size, head_size)
        columns = weight_held[:, pl.ds(first, head_size)]
        for target in range(targets):
            spread_held[target, core] = columns
    spread = pltpu.make_async_copy(spread_held, spread_ref, sems.at[5])
    spread.start()
    out.wait()
    spread.wait()


def copy_kernel(from_ref, to_ref, sem):
    copy = pltpu.make_async_copy(from_ref, to_ref, sem)
    copy.start()
    copy.wait()


def add_pieces(positions, pieces, whole, old_ref):
    owners, _, head_size = old_ref.shape
    xs = owners // 2
    clusters = CLUSTERS
    bf16, f32 = jnp.bfloat16, jnp.float32
    core, x, z = lax.axis_index("core"), lax.axis_index("x"), lax.axis_index("z")
    head = core * xs + x
    heads = whole.shape[0] // (2 * positions)
    first = pl.multiple_of(head * positions, positions)
    second = pl.multiple_of(first + heads * positions, positions)
    cluster = lax.broadcasted_iota(jnp.int32, (clusters, positions), 0).astype(f32)
    mine = (head == z).astype(f32)
    keys, hots = [], []
    for piece, kind, other in pieces:
        key = jnp.dot(piece[:positions, :], whole, preferred_element_type=f32)
        mean = jnp.mean(key * key, axis=1, keepdims=True)
        keys.append((key * lax.rsqrt(mean + EPSILON)).astype(bf16))
        high = piece[positions:, pl.ds(first, positions)].astype(f32)
        low = piece[positions:, pl.ds(second, positions)].astype(f32)
        ids = high[:1] * 32.0 + low[:1]
        hots.append(jnp.where(cluster == ids, 1.0, 0.0).astype(bf16))
        source = 1 - core if other else core
        sign = 2 * source - 1
        moved = (x + (0, sign, -sign, 2)[kind] + xs) % xs
        old_ref[source * xs + moved] = piece[positions:, :head_size].astype(f32) * mine
    one_hot, unit_keys = jnp.concatenate(hots, axis=1), jnp.concatenate(keys, axis=0)
    sums = jnp.dot(one_hot, unit_keys, preferred_element_type=f32)
    counts = lax.dot_general(
        jnp.ones((8, one_hot.shape[1]), bf16), one_hot, (((1,), (1,)), ((), ())),
        preferred_element_type=f32,
    )
    return sums, counts


def near_kernel(positions, *refs):
    arrays, (mine_ref, others_ref, weight_ref, sums_ref, counts_ref, old_ref) = refs[:-6], refs[-6:]
    kinds = len(arrays) // 2
    core = lax.axis_index("core")

    @pl.when(core == 0)
    def _():
        weight_ref[:, 0] = mine_ref[:, 0]
        weight_ref[:, 1] = others_ref[:, 0]

    @pl.when(core == 1)
    def _():
        weight_ref[:, 1] = mine_ref[:, 1]
        weight_ref[:, 0] = others_ref[:, 1]

    whole = weight_ref[...].reshape(arrays[0].shape[1], weight_ref.shape[3])
    pieces = [(piece, number % kinds, number // kinds) for number, piece in enumerate(arrays)]
    old_ref[...] = jnp.zeros_like(old_ref)
    sums_ref[...], counts_ref[...] = add_pieces(positions, pieces, whole, old_ref)


def far_kernel(
    positions, far_ref, over_ref, weight_ref, near_sums_ref, near_counts_ref, near_old_ref,
    out_ref, old_ref,
):
    owners, rows, head_size = out_ref.shape
    block = rows - TILE
    whole = weight_ref[...].reshape(far_ref.shape[1], head_size)
    old_ref[...] = near_old_ref[...]
    pieces = [(far_ref, 3, 0), (over_ref, 3, 1)]
    sums, counts = add_pieces(positions, pieces, whole, old_ref)
    sums += near_sums_ref[...]
    counts = (counts + near_counts_ref[...])[:1]
    empty = jnp.zeros((1, head_size - block), jnp.float32)
    for owner in range(owners):
        own = slice(owner * block, (owner + 1) * block)
        out_ref[owner, :block, :] = sums[own].astype(jnp.bfloat16)
        padded = jnp.concatenate([counts[:, own], empty], axis=1)
        out_ref[owner, block:, :] = count_lines(padded, old_ref[owner]).astype(jnp.bfloat16)


def share_kernel(arrived_ref, out_ref):
    block = arrived_ref.shape[1] - TILE
    bf16, f32 = jnp.bfloat16, jnp.float32
    total = arrived_ref[0].astype(f32)
    for source in range(1, arrived_ref.shape[0]):
        total += arrived_ref[source].astype(f32)
    counts = total[block:block + 1] * COUNT_BASE + total[block + 1:block + 2]
    sums = total[:block].astype(bf16)
    lines = count_lines(counts, total[block:]).astype(bf16)
    for target in range(out_ref.shape[0]):
        out_ref[target, :block, :] = sums
        out_ref[target, block:, :] = lines


def update_kernel(arrived_ref, out_ref):
    sources = arrived_ref.shape[0]
    block = out_ref.shape[1]
    f32 = jnp.float32
    total = arrived_ref[0].astype(f32)
    old = [total[block + OLD_AT:]]
    for source in range(1, sources):
        arrived = arrived_ref[source].astype(f32)
        old.append(arrived[block + OLD_AT:])
        total += arrived
    old = jnp.concatenate(old, axis=0)
    counts = total[block:block + 1, :block] * COUNT_BASE + total[block + 1:block + 2, :block]
    diagonal = lax.broadcasted_iota(jnp.int32, (block, block), 0) == lax.broadcasted_iota(
        jnp.int32, (block, block), 1
    )
    counts = jnp.sum(jnp.where(diagonal, counts, 0.0), axis=1, keepdims=True)
    scaled = total[:block] / jnp.sqrt(jnp.maximum(counts, 1.0))
    mixed = DECAY_RATE * old + (1.0 - DECAY_RATE) * scaled
    mean = jnp.mean(mixed * mixed, axis=1, keepdims=True)
    centroids = (mixed * lax.rsqrt(mean + EPSILON)).astype(jnp.bfloat16)
    for target in range(out_ref.shape[0]):
        out_ref[target] = centroids


def per_device(hidden, key_weight, cluster_ids, old_centroids):
    _, positions, model_width = hidden.shape
    heads = cluster_ids.shape[1]
    head_size = key_weight.shape[1] // heads
    cores, xs, zs = SIZES["core"], SIZES["x"], SIZES["z"]
    ylos = SIZES["ylo"]
    ys = SIZES["yhi"] * ylos
    block = old_centroids.shape[0] * ys
    clusters = block * zs
    bf16, f32 = jnp.bfloat16, jnp.float32

    core = lax.axis_index("core")
    here, spread = pl.pallas_call(
        join_kernel,
        out_shape=(
            jax.ShapeDtypeStruct((positions + TILE, model_width), bf16),
            jax.ShapeDtypeStruct((zs * ylos, cores, key_weight.shape[0], head_size), bf16),
        ),
        in_specs=[ANY] * 4,
        out_specs=(ANY, ANY),
        scratch_shapes=[
            pltpu.VMEM((heads, positions), jnp.int32),
            pltpu.VMEM(old_centroids.shape, f32),
            pltpu.VMEM((positions + TILE, model_width), bf16),
            pltpu.VMEM(key_weight.shape, bf16),
            pltpu.VMEM((zs * ylos, cores, key_weight.shape[0], head_size), bf16),
            pltpu.SemaphoreType.DMA((6,)),
        ],
        compiler_params=ALONE,
    )(
        hidden.reshape(positions, model_width), cluster_ids.reshape(heads, positions),
        old_centroids, key_weight,
    )
    swap = [(0, 1), (1, 0)]
    up = lax.ppermute(here, RING, turn(1))
    down = lax.ppermute(here, RING, turn(-1))
    weight = lax.all_to_all(spread, ("z", "ylo"), split_axis=0, concat_axis=0, tiled=True)
    up, down = lax.optimization_barrier((up, down))
    far = lax.ppermute(up, RING, turn(1))
    near = pl.pallas_call(
        copy_kernel,
        out_shape=jax.ShapeDtypeStruct(here.shape, here.dtype),
        in_specs=[ANY],
        out_specs=ANY,
        scratch_shapes=[pltpu.SemaphoreType.DMA],
        compiler_params=PARAMS,
    )(here)
    near_over = lax.ppermute(near, "core", swap)
    up_over = lax.ppermute(up, "core", swap)
    down_over = lax.ppermute(down, "core", swap)
    weight, near_over = lax.optimization_barrier((weight, near_over))
    others = lax.ppermute(weight, "core", swap)
    far_over = lax.ppermute(far, "core", swap)

    whole, *partial = pl.pallas_call(
        functools.partial(near_kernel, positions),
        out_shape=(
            jax.ShapeDtypeStruct(weight.shape[:3] + (head_size,), bf16),
            jax.ShapeDtypeStruct((clusters, head_size), f32),
            jax.ShapeDtypeStruct((8, clusters), f32),
            jax.ShapeDtypeStruct((zs, TILE, head_size), f32),
        ),
        in_specs=[VMEM] * 8,
        out_specs=(VMEM,) * 4,
        compiler_params=PARAMS,
        cost_estimate=pl.CostEstimate(flops=2 * 10**9, bytes_accessed=6 * 10**6, transcendentals=0),
    )(near, up, down, near_over, up_over, down_over, weight, others)
    payload = pl.pallas_call(
        functools.partial(far_kernel, positions),
        out_shape=jax.ShapeDtypeStruct((zs, block + TILE, head_size), bf16),
        in_specs=[VMEM] * 6,
        out_specs=VMEM,
        scratch_shapes=[pltpu.VMEM((zs, TILE, head_size), f32)],
        compiler_params=PARAMS,
        cost_estimate=pl.CostEstimate(flops=10**9, bytes_accessed=2 * 10**6, transcendentals=0),
    )(far, far_over, whole, *partial)
    arrived = lax.all_to_all(payload, "z", split_axis=0, concat_axis=0, tiled=True)

    shares = pl.pallas_call(
        share_kernel,
        out_shape=jax.ShapeDtypeStruct((ys, block + TILE, head_size), bf16),
        in_specs=[VMEM],
        out_specs=VMEM,
        compiler_params=PARAMS,
    )(arrived)
    arrived = lax.all_to_all(shares, Y, split_axis=0, concat_axis=0, tiled=True)

    owned = pl.pallas_call(
        update_kernel,
        out_shape=jax.ShapeDtypeStruct((xs * zs, block, head_size), bf16),
        in_specs=[VMEM],
        out_specs=VMEM,
        compiler_params=PARAMS,
    )(arrived)
    half = lax.all_to_all(owned, ("x", "z"), split_axis=0, concat_axis=0, tiled=True)
    half = half.reshape(xs, zs, block, head_size)
    other = lax.ppermute(half, "core", swap)
    first = jnp.where(core == 0, half, other)
    second = jnp.where(core == 0, other, half)
    out = jnp.stack([first, second]).reshape(cores, xs, cores, xs, SIZES["yhi"], ylos, 8, head_size)
    out = jnp.transpose(out, (0, 1, 5, 2, 4, 3, 6, 7)).astype(f32)
    return out.reshape(heads * clusters, head_size)


def solution(mesh):
    fine = Mesh(np.asarray(mesh.devices).reshape(tuple(SIZES.values())), AXES)
    ctx, dp = ("z", "ylo", "core"), ("yhi", "x")
    in_specs = (P(dp, ctx, None), P(ctx, None), P(dp, None, ctx), P(ctx + dp, None))
    return jax.shard_map(
        per_device, mesh=fine, in_specs=in_specs, out_specs=P(), check_vma=False
    )
```

```python
import functools

import jax
import jax.numpy as jnp
import numpy as np
from jax import lax
from jax.experimental import pallas as pl
from jax.experimental.pallas import tpu as pltpu
from jax.sharding import Mesh, PartitionSpec as P

EPSILON = 1e-06
DECAY_RATE = 0.5

SIZES = {"z": 8, "ylo": 2, "core": 2, "yhi": 4, "x": 4}
AXES = tuple(SIZES)
RING = ("core", "x")
Y = ("yhi", "ylo")
TILE = 16
COUNT_BASE = 64.0
OLD_AT = 8
CLUSTERS = 512

VMEM = pl.BlockSpec(memory_space=pltpu.VMEM)
ANY = pl.BlockSpec(memory_space=pl.ANY)
ALONE = pltpu.CompilerParams(vmem_limit_bytes=63_200_000)
PARAMS = pltpu.CompilerParams(vmem_limit_bytes=24 * 1024 * 1024)


def turn(step):
    xs = SIZES["x"]
    return [
        (core * xs + x, core * xs + (x + (step if core == 0 else -step)) % xs)
        for core in range(SIZES["core"])
        for x in range(xs)
    ]


def place_of(ids):
    ylo, core = ids >> 8, (ids >> 7) & 1
    yhi, x, row = (ids >> 5) & 3, (ids >> 3) & 3, ids & 7
    return (core * 4 + x) * 64 + (yhi * 2 + ylo) * 8 + row


def block_of(z, y):
    core, x, yhi, ylo = z // 4, z % 4, y // 2, y % 2
    return ylo * 32 + core * 16 + yhi * 4 + x


def count_lines(counts, rest):
    high = jnp.floor(counts * (1.0 / COUNT_BASE))
    low = counts - COUNT_BASE * high
    row = lax.broadcasted_iota(jnp.int32, rest.shape, 0)
    return jnp.where(row == 0, high, jnp.where(row == 1, low, jnp.where(row < OLD_AT, 0.0, rest)))


def join_kernel(
    hidden_ref, ids_ref, old_ref, weight_ref, out_ref, spread_ref,
    ids_held, old_held, held, weight_held, spread_held, sems,
):
    positions = hidden_ref.shape[0]
    targets, cores, _, head_size = spread_ref.shape
    bf16, f32 = jnp.bfloat16, jnp.float32
    xs = weight_ref.shape[1] // (cores * head_size)
    x = lax.axis_index("x")
    moves = [
        pltpu.make_async_copy(ids_ref, ids_held, sems.at[0]),
        pltpu.make_async_copy(old_ref, old_held, sems.at[1]),
        pltpu.make_async_copy(weight_ref, weight_held, sems.at[2]),
        pltpu.make_async_copy(hidden_ref, held.at[pl.ds(0, positions)], sems.at[3]),
    ]
    for move in moves:
        move.start()
    moves[0].wait()
    moves[1].wait()
    place = place_of(ids_held[...])
    heads, width = place.shape
    parts = ((place >> 5).astype(f32), (place & 31).astype(f32))
    row = lax.broadcasted_iota(jnp.int32, (OLD_AT, width), 0)
    old = old_held[...]
    for number in range(2 * heads):
        part, head = divmod(number, heads)
        line = jnp.where(row == 0, parts[part][head:head + 1], 0.0)
        rest = old if number == 0 else jnp.zeros_like(old)
        lines = jnp.concatenate([line, rest], axis=0).astype(bf16)
        held[positions:, number * width:(number + 1) * width] = lines
    moves[3].wait()
    out = pltpu.make_async_copy(held, out_ref, sems.at[4])
    out.start()
    moves[2].wait()
    for core in range(cores):
        first = pl.multiple_of((core * xs + x) * head_size, head_size)
        columns = weight_held[:, pl.ds(first, head_size)]
        for target in range(targets):
            spread_held[target, core] = columns
    spread = pltpu.make_async_copy(spread_held, spread_ref, sems.at[5])
    spread.start()
    out.wait()
    spread.wait()


def copy_kernel(from_ref, to_ref, sem):
    copy = pltpu.make_async_copy(from_ref, to_ref, sem)
    copy.start()
    copy.wait()


def add_pieces(positions, pieces, whole, old_ref):
    owners, _, head_size = old_ref.shape
    xs = owners // 2
    clusters = CLUSTERS
    bf16, f32 = jnp.bfloat16, jnp.float32
    core, x, z = lax.axis_index("core"), lax.axis_index("x"), lax.axis_index("z")
    head = core * xs + x
    heads = whole.shape[0] // (2 * positions)
    first = pl.multiple_of(head * positions, positions)
    second = pl.multiple_of(first + heads * positions, positions)
    cluster = lax.broadcasted_iota(jnp.int32, (clusters, positions), 0).astype(f32)
    mine = (head == z).astype(f32)
    keys, hots = [], []
    for piece, kind, other, move in pieces:
        if move is not None:
            move.wait()
        key = jnp.dot(piece[:positions, :], whole, preferred_element_type=f32)
        mean = jnp.mean(key * key, axis=1, keepdims=True)
        keys.append((key * lax.rsqrt(mean + EPSILON)).astype(bf16))
        high = piece[positions:, pl.ds(first, positions)].astype(f32)
        low = piece[positions:, pl.ds(second, positions)].astype(f32)
        ids = high[:1] * 32.0 + low[:1]
        hots.append(jnp.where(cluster == ids, 1.0, 0.0).astype(bf16))
        source = 1 - core if other else core
        sign = 2 * source - 1
        moved = (x + (0, sign, -sign, 2)[kind] + xs) % xs
        old_ref[source * xs + moved] = piece[positions:, :head_size].astype(f32) * mine
    one_hot, unit_keys = jnp.concatenate(hots, axis=1), jnp.concatenate(keys, axis=0)
    sums = jnp.dot(one_hot, unit_keys, preferred_element_type=f32)
    counts = lax.dot_general(
        jnp.ones((8, one_hot.shape[1]), bf16), one_hot, (((1,), (1,)), ((), ())),
        preferred_element_type=f32,
    )
    return sums, counts


def near_kernel(positions, *refs):
    arrays, (mine_ref, others_ref, weight_ref, sums_ref, counts_ref, old_ref) = refs[:6], refs[6:12]
    held, sems = refs[12:]
    kinds = len(arrays) // 2
    late = len(arrays) - held.shape[0]
    moves = [None] * late + [
        pltpu.make_async_copy(arrays[late + number], held.at[number], sems.at[number])
        for number in range(held.shape[0])
    ]
    for move in moves[late:]:
        move.start()
    core = lax.axis_index("core")

    @pl.when(core == 0)
    def _():
        weight_ref[:, 0] = mine_ref[:, 0]
        weight_ref[:, 1] = others_ref[:, 0]

    @pl.when(core == 1)
    def _():
        weight_ref[:, 1] = mine_ref[:, 1]
        weight_ref[:, 0] = others_ref[:, 1]

    whole = weight_ref[...].reshape(arrays[0].shape[1], weight_ref.shape[3])
    arrays = list(arrays[:late]) + [held.at[number] for number in range(held.shape[0])]
    pieces = [
        (piece, number % kinds, number // kinds, move)
        for number, (piece, move) in enumerate(zip(arrays, moves))
    ]
    old_ref[...] = jnp.zeros_like(old_ref)
    sums_ref[...], counts_ref[...] = add_pieces(positions, pieces, whole, old_ref)


def far_kernel(
    positions, far_ref, over_ref, weight_ref, near_sums_ref, near_counts_ref, near_old_ref,
    out_ref, old_ref,
):
    owners, rows, head_size = out_ref.shape
    block = rows - TILE
    whole = weight_ref[...].reshape(far_ref.shape[1], head_size)
    old_ref[...] = near_old_ref[...]
    pieces = [(far_ref, 3, 0, None), (over_ref, 3, 1, None)]
    sums, counts = add_pieces(positions, pieces, whole, old_ref)
    sums += near_sums_ref[...]
    counts = (counts + near_counts_ref[...])[:1]
    empty = jnp.zeros((1, head_size - block), jnp.float32)
    for owner in range(owners):
        own = slice(owner * block, (owner + 1) * block)
        out_ref[owner, :block, :] = sums[own].astype(jnp.bfloat16)
        padded = jnp.concatenate([counts[:, own], empty], axis=1)
        out_ref[owner, block:, :] = count_lines(padded, old_ref[owner]).astype(jnp.bfloat16)


def share_kernel(arrived_ref, out_ref):
    block = arrived_ref.shape[1] - TILE
    bf16, f32 = jnp.bfloat16, jnp.float32
    total = arrived_ref[0].astype(f32)
    for source in range(1, arrived_ref.shape[0]):
        total += arrived_ref[source].astype(f32)
    counts = total[block:block + 1] * COUNT_BASE + total[block + 1:block + 2]
    sums = total[:block].astype(bf16)
    lines = count_lines(counts, total[block:]).astype(bf16)
    for target in range(out_ref.shape[0]):
        out_ref[target, :block, :] = sums
        out_ref[target, block:, :] = lines


def update_kernel(arrived_ref, out_ref):
    sources = arrived_ref.shape[0]
    block = out_ref.shape[1]
    f32 = jnp.float32
    total = arrived_ref[0].astype(f32)
    old = [total[block + OLD_AT:]]
    for source in range(1, sources):
        arrived = arrived_ref[source].astype(f32)
        old.append(arrived[block + OLD_AT:])
        total += arrived
    old = jnp.concatenate(old, axis=0)
    counts = total[block:block + 1, :block] * COUNT_BASE + total[block + 1:block + 2, :block]
    diagonal = lax.broadcasted_iota(jnp.int32, (block, block), 0) == lax.broadcasted_iota(
        jnp.int32, (block, block), 1
    )
    counts = jnp.sum(jnp.where(diagonal, counts, 0.0), axis=1, keepdims=True)
    scaled = total[:block] / jnp.sqrt(jnp.maximum(counts, 1.0))
    mixed = DECAY_RATE * old + (1.0 - DECAY_RATE) * scaled
    mean = jnp.mean(mixed * mixed, axis=1, keepdims=True)
    centroids = (mixed * lax.rsqrt(mean + EPSILON)).astype(jnp.bfloat16)
    for target in range(out_ref.shape[0]):
        out_ref[target] = centroids


def per_device(hidden, key_weight, cluster_ids, old_centroids):
    _, positions, model_width = hidden.shape
    heads = cluster_ids.shape[1]
    head_size = key_weight.shape[1] // heads
    cores, xs, zs = SIZES["core"], SIZES["x"], SIZES["z"]
    ylos = SIZES["ylo"]
    ys = SIZES["yhi"] * ylos
    block = old_centroids.shape[0] * ys
    clusters = block * zs
    bf16, f32 = jnp.bfloat16, jnp.float32

    core = lax.axis_index("core")
    here, spread = pl.pallas_call(
        join_kernel,
        out_shape=(
            jax.ShapeDtypeStruct((positions + TILE, model_width), bf16),
            jax.ShapeDtypeStruct((zs * ylos, cores, key_weight.shape[0], head_size), bf16),
        ),
        in_specs=[ANY] * 4,
        out_specs=(ANY, ANY),
        scratch_shapes=[
            pltpu.VMEM((heads, positions), jnp.int32),
            pltpu.VMEM(old_centroids.shape, f32),
            pltpu.VMEM((positions + TILE, model_width), bf16),
            pltpu.VMEM(key_weight.shape, bf16),
            pltpu.VMEM((zs * ylos, cores, key_weight.shape[0], head_size), bf16),
            pltpu.SemaphoreType.DMA((6,)),
        ],
        compiler_params=ALONE,
    )(
        hidden.reshape(positions, model_width), cluster_ids.reshape(heads, positions),
        old_centroids, key_weight,
    )
    swap = [(0, 1), (1, 0)]
    up = lax.ppermute(here, RING, turn(1))
    down = lax.ppermute(here, RING, turn(-1))
    weight = lax.all_to_all(spread, ("z", "ylo"), split_axis=0, concat_axis=0, tiled=True)
    far = lax.ppermute(up, RING, turn(1))
    near = pl.pallas_call(
        copy_kernel,
        out_shape=jax.ShapeDtypeStruct(here.shape, here.dtype),
        in_specs=[ANY],
        out_specs=ANY,
        scratch_shapes=[pltpu.SemaphoreType.DMA],
        compiler_params=PARAMS,
    )(here)
    near_over = lax.ppermute(near, "core", swap)
    up_over = lax.ppermute(up, "core", swap)
    down_over = lax.ppermute(down, "core", swap)
    weight, near_over = lax.optimization_barrier((weight, near_over))
    others = lax.ppermute(weight, "core", swap)
    far, down_over = lax.optimization_barrier((far, down_over))
    far_over = lax.ppermute(far, "core", swap)

    whole, *partial = pl.pallas_call(
        functools.partial(near_kernel, positions),
        out_shape=(
            jax.ShapeDtypeStruct(weight.shape[:3] + (head_size,), bf16),
            jax.ShapeDtypeStruct((clusters, head_size), f32),
            jax.ShapeDtypeStruct((8, clusters), f32),
            jax.ShapeDtypeStruct((zs, TILE, head_size), f32),
        ),
        in_specs=[VMEM] * 4 + [ANY] * 2 + [VMEM] * 2,
        out_specs=(VMEM,) * 4,
        scratch_shapes=[pltpu.VMEM((2,) + here.shape, bf16), pltpu.SemaphoreType.DMA((2,))],
        compiler_params=PARAMS,
        cost_estimate=pl.CostEstimate(flops=2 * 10**9, bytes_accessed=6 * 10**6, transcendentals=0),
    )(near, up, down, near_over, up_over, down_over, weight, others)
    payload = pl.pallas_call(
        functools.partial(far_kernel, positions),
        out_shape=jax.ShapeDtypeStruct((zs, block + TILE, head_size), bf16),
        in_specs=[VMEM] * 6,
        out_specs=VMEM,
        scratch_shapes=[pltpu.VMEM((zs, TILE, head_size), f32)],
        compiler_params=PARAMS,
        cost_estimate=pl.CostEstimate(flops=10**9, bytes_accessed=2 * 10**6, transcendentals=0),
    )(far, far_over, whole, *partial)
    arrived = lax.all_to_all(payload, "z", split_axis=0, concat_axis=0, tiled=True)

    shares = pl.pallas_call(
        share_kernel,
        out_shape=jax.ShapeDtypeStruct((ys, block + TILE, head_size), bf16),
        in_specs=[VMEM],
        out_specs=VMEM,
        compiler_params=PARAMS,
    )(arrived)
    arrived = lax.all_to_all(shares, Y, split_axis=0, concat_axis=0, tiled=True)

    owned = pl.pallas_call(
        update_kernel,
        out_shape=jax.ShapeDtypeStruct((xs * zs, block, head_size), bf16),
        in_specs=[VMEM],
        out_specs=VMEM,
        compiler_params=PARAMS,
    )(arrived)
    half = lax.all_to_all(owned, ("x", "z"), split_axis=0, concat_axis=0, tiled=True)
    half = half.reshape(xs, zs, block, head_size)
    other = lax.ppermute(half, "core", swap)
    first = jnp.where(core == 0, half, other)
    second = jnp.where(core == 0, other, half)
    out = jnp.stack([first, second]).reshape(cores, xs, cores, xs, SIZES["yhi"], ylos, 8, head_size)
    out = jnp.transpose(out, (0, 1, 5, 2, 4, 3, 6, 7)).astype(f32)
    return out.reshape(heads * clusters, head_size)


def solution(mesh):
    fine = Mesh(np.asarray(mesh.devices).reshape(tuple(SIZES.values())), AXES)
    ctx, dp = ("z", "ylo", "core"), ("yhi", "x")
    in_specs = (P(dp, ctx, None), P(ctx, None), P(dp, None, ctx), P(ctx + dp, None))
    return jax.shard_map(
        per_device, mesh=fine, in_specs=in_specs, out_specs=P(), check_vma=False
    )
```

```python
import functools

import jax
import jax.numpy as jnp
import numpy as np
from jax import lax
from jax.experimental import pallas as pl
from jax.experimental.pallas import tpu as pltpu
from jax.sharding import Mesh, PartitionSpec as P

EPSILON = 1e-06
DECAY_RATE = 0.5

SIZES = {"z": 8, "ylo": 2, "core": 2, "yhi": 4, "x": 4}
AXES = tuple(SIZES)
RING = ("core", "x")
Y = ("yhi", "ylo")
TILE = 16
COUNT_BASE = 64.0
OLD_AT = 8
CLUSTERS = 512

VMEM = pl.BlockSpec(memory_space=pltpu.VMEM)
ANY = pl.BlockSpec(memory_space=pl.ANY)
ALONE = pltpu.CompilerParams(vmem_limit_bytes=63_200_000)
PARAMS = pltpu.CompilerParams(vmem_limit_bytes=24 * 1024 * 1024)


def turn(step):
    xs = SIZES["x"]
    return [
        (core * xs + x, core * xs + (x + (step if core == 0 else -step)) % xs)
        for core in range(SIZES["core"])
        for x in range(xs)
    ]


def place_of(ids):
    ylo, core = ids >> 8, (ids >> 7) & 1
    yhi, x, row = (ids >> 5) & 3, (ids >> 3) & 3, ids & 7
    return (core * 4 + x) * 64 + (yhi * 2 + ylo) * 8 + row


def block_of(z, y):
    core, x, yhi, ylo = z // 4, z % 4, y // 2, y % 2
    return ylo * 32 + core * 16 + yhi * 4 + x


def count_lines(counts, rest):
    high = jnp.floor(counts * (1.0 / COUNT_BASE))
    low = counts - COUNT_BASE * high
    row = lax.broadcasted_iota(jnp.int32, rest.shape, 0)
    return jnp.where(row == 0, high, jnp.where(row == 1, low, jnp.where(row < OLD_AT, 0.0, rest)))


def join_kernel(
    hidden_ref, ids_ref, old_ref, weight_ref, out_ref, spread_ref,
    ids_held, old_held, held, weight_held, spread_held, sems,
):
    positions = hidden_ref.shape[0]
    targets, cores, _, head_size = spread_ref.shape
    bf16, f32 = jnp.bfloat16, jnp.float32
    xs = weight_ref.shape[1] // (cores * head_size)
    x = lax.axis_index("x")
    moves = [
        pltpu.make_async_copy(ids_ref, ids_held, sems.at[0]),
        pltpu.make_async_copy(old_ref, old_held, sems.at[1]),
        pltpu.make_async_copy(weight_ref, weight_held, sems.at[2]),
        pltpu.make_async_copy(hidden_ref, held.at[pl.ds(0, positions)], sems.at[3]),
    ]
    for move in moves:
        move.start()
    moves[0].wait()
    moves[1].wait()
    place = place_of(ids_held[...])
    heads, width = place.shape
    parts = ((place >> 5).astype(f32), (place & 31).astype(f32))
    row = lax.broadcasted_iota(jnp.int32, (OLD_AT, width), 0)
    old = old_held[...]
    for number in range(2 * heads):
        part, head = divmod(number, heads)
        line = jnp.where(row == 0, parts[part][head:head + 1], 0.0)
        rest = old if number == 0 else jnp.zeros_like(old)
        lines = jnp.concatenate([line, rest], axis=0).astype(bf16)
        held[positions:, number * width:(number + 1) * width] = lines
    moves[3].wait()
    out = pltpu.make_async_copy(held, out_ref, sems.at[4])
    out.start()
    moves[2].wait()
    for core in range(cores):
        first = pl.multiple_of((core * xs + x) * head_size, head_size)
        columns = weight_held[:, pl.ds(first, head_size)]
        for target in range(targets):
            spread_held[target, core] = columns
    spread = pltpu.make_async_copy(spread_held, spread_ref, sems.at[5])
    spread.start()
    out.wait()
    spread.wait()


def copy_kernel(from_ref, to_ref, sem):
    copy = pltpu.make_async_copy(from_ref, to_ref, sem)
    copy.start()
    copy.wait()


def add_pieces(positions, pieces, whole, old_ref):
    owners, _, head_size = old_ref.shape
    xs = owners // 2
    clusters = CLUSTERS
    bf16, f32 = jnp.bfloat16, jnp.float32
    core, x, z = lax.axis_index("core"), lax.axis_index("x"), lax.axis_index("z")
    head = core * xs + x
    heads = whole.shape[0] // (2 * positions)
    first = pl.multiple_of(head * positions, positions)
    second = pl.multiple_of(first + heads * positions, positions)
    cluster = lax.broadcasted_iota(jnp.int32, (clusters, positions), 0).astype(f32)
    mine = (head == z).astype(f32)
    keys, hots = [], []
    for piece, kind, other, move in pieces:
        if move is not None:
            move.wait()
        key = jnp.dot(piece[:positions, :], whole, preferred_element_type=f32)
        mean = jnp.mean(key * key, axis=1, keepdims=True)
        keys.append((key * lax.rsqrt(mean + EPSILON)).astype(bf16))
        high = piece[positions:, pl.ds(first, positions)].astype(f32)
        low = piece[positions:, pl.ds(second, positions)].astype(f32)
        ids = high[:1] * 32.0 + low[:1]
        hots.append(jnp.where(cluster == ids, 1.0, 0.0).astype(bf16))
        source = 1 - core if other else core
        sign = 2 * source - 1
        moved = (x + (0, sign, -sign, 2)[kind] + xs) % xs
        old_ref[source * xs + moved] = piece[positions:, :head_size].astype(f32) * mine
    one_hot, unit_keys = jnp.concatenate(hots, axis=1), jnp.concatenate(keys, axis=0)
    sums = jnp.dot(one_hot, unit_keys, preferred_element_type=f32)
    counts = lax.dot_general(
        jnp.ones((8, one_hot.shape[1]), bf16), one_hot, (((1,), (1,)), ((), ())),
        preferred_element_type=f32,
    )
    return sums, counts


def near_kernel(positions, *refs):
    arrays, (mine_ref, others_ref, weight_ref, sums_ref, counts_ref, old_ref) = refs[:6], refs[6:12]
    held, sems = refs[12:]
    kinds = len(arrays) // 2
    late = len(arrays) - held.shape[0]
    moves = [None] * late + [
        pltpu.make_async_copy(arrays[late + number], held.at[number], sems.at[number])
        for number in range(held.shape[0])
    ]
    for move in moves[late:]:
        move.start()
    core = lax.axis_index("core")

    @pl.when(core == 0)
    def _():
        weight_ref[:, 0] = mine_ref[:, 0]
        weight_ref[:, 1] = others_ref[:, 0]

    @pl.when(core == 1)
    def _():
        weight_ref[:, 1] = mine_ref[:, 1]
        weight_ref[:, 0] = others_ref[:, 1]

    whole = weight_ref[...].reshape(arrays[0].shape[1], weight_ref.shape[3])
    arrays = list(arrays[:late]) + [held.at[number] for number in range(held.shape[0])]
    pieces = [
        (piece, number % kinds, number // kinds, move)
        for number, (piece, move) in enumerate(zip(arrays, moves))
    ]
    old_ref[...] = jnp.zeros_like(old_ref)
    sums_ref[...], counts_ref[...] = add_pieces(positions, pieces, whole, old_ref)


def far_kernel(
    positions, far_ref, over_ref, weight_ref, near_sums_ref, near_counts_ref, near_old_ref,
    out_ref, old_ref,
):
    owners, rows, head_size = out_ref.shape
    block = rows - TILE
    whole = weight_ref[...].reshape(far_ref.shape[1], head_size)
    old_ref[...] = near_old_ref[...]
    pieces = [(far_ref, 3, 0, None), (over_ref, 3, 1, None)]
    sums, counts = add_pieces(positions, pieces, whole, old_ref)
    sums += near_sums_ref[...]
    counts = (counts + near_counts_ref[...])[:1]
    empty = jnp.zeros((1, head_size - block), jnp.float32)
    for owner in range(owners):
        own = slice(owner * block, (owner + 1) * block)
        out_ref[owner, :block, :] = sums[own].astype(jnp.bfloat16)
        padded = jnp.concatenate([counts[:, own], empty], axis=1)
        out_ref[owner, block:, :] = count_lines(padded, old_ref[owner]).astype(jnp.bfloat16)


def share_kernel(arrived_ref, out_ref):
    block = arrived_ref.shape[1] - TILE
    bf16, f32 = jnp.bfloat16, jnp.float32
    total = arrived_ref[0].astype(f32)
    for source in range(1, arrived_ref.shape[0]):
        total += arrived_ref[source].astype(f32)
    counts = total[block:block + 1] * COUNT_BASE + total[block + 1:block + 2]
    sums = total[:block].astype(bf16)
    lines = count_lines(counts, total[block:]).astype(bf16)
    for target in range(out_ref.shape[0]):
        out_ref[target, :block, :] = sums
        out_ref[target, block:, :] = lines


def update_kernel(arrived_ref, out_ref):
    sources = arrived_ref.shape[0]
    block = out_ref.shape[1]
    f32 = jnp.float32
    total = arrived_ref[0].astype(f32)
    old = [total[block + OLD_AT:]]
    for source in range(1, sources):
        arrived = arrived_ref[source].astype(f32)
        old.append(arrived[block + OLD_AT:])
        total += arrived
    old = jnp.concatenate(old, axis=0)
    counts = total[block:block + 1, :block] * COUNT_BASE + total[block + 1:block + 2, :block]
    diagonal = lax.broadcasted_iota(jnp.int32, (block, block), 0) == lax.broadcasted_iota(
        jnp.int32, (block, block), 1
    )
    counts = jnp.sum(jnp.where(diagonal, counts, 0.0), axis=1, keepdims=True)
    scaled = total[:block] / jnp.sqrt(jnp.maximum(counts, 1.0))
    mixed = DECAY_RATE * old + (1.0 - DECAY_RATE) * scaled
    mean = jnp.mean(mixed * mixed, axis=1, keepdims=True)
    centroids = (mixed * lax.rsqrt(mean + EPSILON)).astype(jnp.bfloat16)
    for target in range(out_ref.shape[0]):
        out_ref[target] = centroids


def per_device(hidden, key_weight, cluster_ids, old_centroids):
    _, positions, model_width = hidden.shape
    heads = cluster_ids.shape[1]
    head_size = key_weight.shape[1] // heads
    cores, xs, zs = SIZES["core"], SIZES["x"], SIZES["z"]
    ylos = SIZES["ylo"]
    ys = SIZES["yhi"] * ylos
    block = old_centroids.shape[0] * ys
    clusters = block * zs
    bf16, f32 = jnp.bfloat16, jnp.float32

    core = lax.axis_index("core")
    here, spread = pl.pallas_call(
        join_kernel,
        out_shape=(
            jax.ShapeDtypeStruct((positions + TILE, model_width), bf16),
            jax.ShapeDtypeStruct((zs * ylos, cores, key_weight.shape[0], head_size), bf16),
        ),
        in_specs=[ANY] * 4,
        out_specs=(ANY, ANY),
        scratch_shapes=[
            pltpu.VMEM((heads, positions), jnp.int32),
            pltpu.VMEM(old_centroids.shape, f32),
            pltpu.VMEM((positions + TILE, model_width), bf16),
            pltpu.VMEM(key_weight.shape, bf16),
            pltpu.VMEM((zs * ylos, cores, key_weight.shape[0], head_size), bf16),
            pltpu.SemaphoreType.DMA((6,)),
        ],
        compiler_params=ALONE,
    )(
        hidden.reshape(positions, model_width), cluster_ids.reshape(heads, positions),
        old_centroids, key_weight,
    )
    swap = [(0, 1), (1, 0)]
    up = lax.ppermute(here, RING, turn(1))
    down = lax.ppermute(here, RING, turn(-1))
    weight = lax.all_to_all(spread, ("z", "ylo"), split_axis=0, concat_axis=0, tiled=True)
    far = lax.ppermute(up, RING, turn(1))
    near = pl.pallas_call(
        copy_kernel,
        out_shape=jax.ShapeDtypeStruct(here.shape, here.dtype),
        in_specs=[ANY],
        out_specs=ANY,
        scratch_shapes=[pltpu.SemaphoreType.DMA],
        compiler_params=PARAMS,
    )(here)
    near_over = lax.ppermute(near, "core", swap)
    up_over = lax.ppermute(up, "core", swap)
    down_over = lax.ppermute(down, "core", swap)
    weight, near_over = lax.optimization_barrier((weight, near_over))
    others = lax.ppermute(weight, "core", swap)
    far, down_over, up_over = lax.optimization_barrier((far, down_over, up_over))
    far_over = lax.ppermute(far, "core", swap)

    whole, *partial = pl.pallas_call(
        functools.partial(near_kernel, positions),
        out_shape=(
            jax.ShapeDtypeStruct(weight.shape[:3] + (head_size,), bf16),
            jax.ShapeDtypeStruct((clusters, head_size), f32),
            jax.ShapeDtypeStruct((8, clusters), f32),
            jax.ShapeDtypeStruct((zs, TILE, head_size), f32),
        ),
        in_specs=[VMEM] * 4 + [ANY] * 2 + [VMEM] * 2,
        out_specs=(VMEM,) * 4,
        scratch_shapes=[pltpu.VMEM((2,) + here.shape, bf16), pltpu.SemaphoreType.DMA((2,))],
        compiler_params=PARAMS,
        cost_estimate=pl.CostEstimate(flops=2 * 10**9, bytes_accessed=6 * 10**6, transcendentals=0),
    )(near, up, down, near_over, up_over, down_over, weight, others)
    payload = pl.pallas_call(
        functools.partial(far_kernel, positions),
        out_shape=jax.ShapeDtypeStruct((zs, block + TILE, head_size), bf16),
        in_specs=[VMEM] * 6,
        out_specs=VMEM,
        scratch_shapes=[pltpu.VMEM((zs, TILE, head_size), f32)],
        compiler_params=PARAMS,
        cost_estimate=pl.CostEstimate(flops=10**9, bytes_accessed=2 * 10**6, transcendentals=0),
    )(far, far_over, whole, *partial)
    arrived = lax.all_to_all(payload, "z", split_axis=0, concat_axis=0, tiled=True)

    shares = pl.pallas_call(
        share_kernel,
        out_shape=jax.ShapeDtypeStruct((ys, block + TILE, head_size), bf16),
        in_specs=[VMEM],
        out_specs=VMEM,
        compiler_params=PARAMS,
    )(arrived)
    arrived = lax.all_to_all(shares, Y, split_axis=0, concat_axis=0, tiled=True)

    owned = pl.pallas_call(
        update_kernel,
        out_shape=jax.ShapeDtypeStruct((xs * zs, block, head_size), bf16),
        in_specs=[VMEM],
        out_specs=VMEM,
        compiler_params=PARAMS,
    )(arrived)
    half = lax.all_to_all(owned, ("x", "z"), split_axis=0, concat_axis=0, tiled=True)
    half = half.reshape(xs, zs, block, head_size)
    other = lax.ppermute(half, "core", swap)
    first = jnp.where(core == 0, half, other)
    second = jnp.where(core == 0, other, half)
    out = jnp.stack([first, second]).reshape(cores, xs, cores, xs, SIZES["yhi"], ylos, 8, head_size)
    out = jnp.transpose(out, (0, 1, 5, 2, 4, 3, 6, 7)).astype(f32)
    return out.reshape(heads * clusters, head_size)


def solution(mesh):
    fine = Mesh(np.asarray(mesh.devices).reshape(tuple(SIZES.values())), AXES)
    ctx, dp = ("z", "ylo", "core"), ("yhi", "x")
    in_specs = (P(dp, ctx, None), P(ctx, None), P(dp, None, ctx), P(ctx + dp, None))
    return jax.shard_map(
        per_device, mesh=fine, in_specs=in_specs, out_specs=P(), check_vma=False
    )
```
